32 devices in a mesh: view: 4 (over y, x), tm: 8 (over z, core).
Axes of the slice: x: 2, y: 2, z: 4, core: 2. Of those that a mesh axis runs over, the one named last changes fastest.
Arguments:
- frames: bfloat16 [4, 8192, 768], P('view', 'tm'), may hold values from -100 to 100
- conv_weight: bfloat16 [3, 768, 768], replicated, may hold values from -0.125 to 0.125
- conv_bias: float32 [768], replicated, may hold values from -4 to 4
- proj_weight: bfloat16 [768, 768], replicated, may hold values from -0.21875 to 0.21875
- frames_before: int32 [8192], P('tm'), may hold values from -1 to 1023, as said below
- frames_after: int32 [8192], P('tm'), may hold values from -1 to 1023, as said below
Outputs:
- whitened: float32 [4, 8192, 768], P('view', 'tm')
- pair_loss: float32 [4, 8192], P('view', 'tm')
The draws below stay inside these ranges and needn't reach their ends.
Inputs may be any that keep to these rules, and one draw needn't show every extreme that they name: Live frames (frames_before >= 0) form clips of consecutive frames, each at most 1024 frames long; inside a clip frames_before counts up from 0 and frames_after counts down to 0; padding frames carry -1 in both lists, and the first and last frames of the timeline are live. `frames_after`: consistent with frames_before, as stated there.
All inputs are finite; a program needn't handle non-finite values.
Results may differ from the reference program's by a relative error of at most 0.0045.
Values may be sent and summed in bfloat16 or wider, within the bound.
A program may use at most 128 MiB of HBM per device.

```python
import jax
import jax.numpy as jnp
from jax import lax

C = 768
E = 768
DILATION_STEP = 4
F = 1024
TOTAL_FRAMES = 8192
VIEWS = 4


def clip_layout(key):
    steps = jnp.arange(TOTAL_FRAMES, dtype=jnp.int32)
    blocks = TOTAL_FRAMES // F
    denom = max(blocks - 1, 1)
    block_index = steps // F
    within = steps % F
    padding = 2 * F // 3 * (blocks - 1 - block_index) // denom
    pad_start = (F - padding) // 2
    live = jnp.logical_not((within >= pad_start) & (within < pad_start + padding))
    last_start = TOTAL_FRAMES - F
    breaks = (jax.random.randint(key, (TOTAL_FRAMES,), 0, max(F // 2, 2)) == 0) & (steps < last_start)
    forced = (within == F // 2) & (steps < last_start) | (steps == last_start)
    prev_live = jnp.concatenate([jnp.zeros((1,), bool), live[:-1]])
    starts = live & ((steps == 0) | breaks | forced | jnp.logical_not(prev_live))
    next_live = jnp.concatenate([live[1:], jnp.zeros((1,), bool)])
    next_start = jnp.concatenate([starts[1:], jnp.ones((1,), bool)])
    ends = live & (jnp.logical_not(next_live) | next_start)
    start_pos = lax.cummax(jnp.where(starts, steps, 0), axis=0)
    end_pos = lax.cummin(jnp.where(ends, steps, TOTAL_FRAMES), axis=0, reverse=True)
    before = jnp.where(live, steps - start_pos, -1).astype(jnp.int32)
    after = jnp.where(live, end_pos - steps, -1).astype(jnp.int32)
    return (before, after)


def draw_frames_before(key, part):
    return clip_layout(jax.random.fold_in(key, 11))[0]


def draw_frames_after(key, part):
    return clip_layout(jax.random.fold_in(key, 11))[1]


def draw_frames(key, part):
    key_shared, key_view, key_scale = jax.random.split(key, 3)
    shared = jnp.clip(jax.random.normal(key_shared, (1, TOTAL_FRAMES, C), jnp.float32), -4.0, 4.0)
    noise = jnp.clip(jax.random.normal(key_view, (VIEWS, TOTAL_FRAMES, C), jnp.float32), -4.0, 4.0)
    base = shared + 0.5 * noise
    scale = 0.5 * jnp.exp(jax.random.uniform(key_scale, (VIEWS, TOTAL_FRAMES, 1), jnp.float32, 0.0, 2.302585))
    return (base * scale).astype(jnp.bfloat16)


def scatter_about(own_key, extent, scale, bound, kind=jnp.bfloat16):
    array = jax.random.normal(own_key, extent, jnp.float32) * scale
    return jnp.minimum(jnp.maximum(array, -bound), bound).astype(kind)


def setup_inputs(seed: int = 0) -> dict:
    arg_keys = jax.random.split(jax.random.key(seed), 7)
    frames = draw_frames(jax.random.fold_in(arg_keys[6], 71), 0)
    conv_weight = scatter_about(arg_keys[1], (3, C, C), (3 * C) ** -0.5, 0.125)
    conv_bias = scatter_about(arg_keys[2], (C,), 0.7, 4.0, jnp.float32)
    proj_weight = scatter_about(arg_keys[3], (C, E), C ** -0.5, 0.21875)
    frames_before = draw_frames_before(jax.random.fold_in(arg_keys[6], 71), 0)
    frames_after = draw_frames_after(jax.random.fold_in(arg_keys[6], 71), 0)
    return dict(frames=frames, conv_weight=conv_weight, conv_bias=conv_bias, proj_weight=proj_weight, frames_before=frames_before, frames_after=frames_after)


eps_shrink = 0.001

def one_view(input_rows, conv_weight, conv_bias, proj_weight, live, valids):
    padded_input = jnp.pad(input_rows, ((DILATION_STEP, DILATION_STEP), (0, 0)))
    total = jnp.zeros((TOTAL_FRAMES, C), jnp.float32)
    for frame_index in range(3):
        shift_amount = (frame_index - 1) * DILATION_STEP
        shifted_input = padded_input[DILATION_STEP + shift_amount:DILATION_STEP + shift_amount + TOTAL_FRAMES]
        term = jnp.dot(shifted_input.astype(jnp.float32), conv_weight[frame_index].astype(jnp.float32), preferred_element_type=jnp.float32)
        total = total + valids[frame_index][:, None] * term
    hidden = (live[:, None] * jax.nn.gelu(total + conv_bias[None, :], approximate=True)).astype(jnp.bfloat16)
    embed = jnp.dot(hidden.astype(jnp.float32), proj_weight.astype(jnp.float32), preferred_element_type=jnp.float32)
    count = jnp.sum(live)
    mean = jnp.sum(embed, axis=0) / count
    centered = live[:, None] * (embed - mean[None, :])
    gram = jnp.dot(centered.T.astype(jnp.float32), centered.astype(jnp.float32), precision=lax.Precision.HIGHEST, preferred_element_type=jnp.float32)
    cov = gram / count + eps_shrink * jnp.eye(E, dtype=jnp.float32)
    factor = jnp.linalg.cholesky(cov)
    solved = jax.scipy.linalg.solve_triangular(factor, centered.T, lower=True)
    return solved.T

def reference(frames, conv_weight, conv_bias, proj_weight, frames_before, frames_after):
    live = (frames_before >= 0).astype(jnp.float32)
    valids = []
    for frame_index in range(3):
        shift_amount = (frame_index - 1) * DILATION_STEP
        valids.append(((frames_before >= -shift_amount) & (frames_after >= shift_amount)).astype(jnp.float32))
    outputs = []
    for view_index in range(VIEWS):
        outputs.append(one_view(frames[view_index], conv_weight, conv_bias, proj_weight, live, valids))
    whitened = jnp.stack(outputs, axis=0)
    losses = []
    for view_index in range(VIEWS):
        partner = whitened[view_index ^ 1]
        diff = whitened[view_index] - partner
        losses.append(jnp.sum(diff * diff, axis=1) / E)
    pair_loss = jnp.stack(losses, axis=0)
    return (whitened, pair_loss)
```

```python
import functools

import jax
import jax.numpy as jnp
from jax import lax
from jax.experimental import pallas as pl
from jax.experimental.pallas import tpu as pltpu
from jax.sharding import PartitionSpec as P

DILATION_STEP = 4
eps_shrink = 0.001
B = 128
R = 8
HIGHEST = lax.Precision.HIGHEST
NT = (((1,), (1,)), ((), ()))
NN = (((1,), (0,)), ((), ()))
TN = (((0,), (0,)), ((), ()))


def dot(a, b, dims, precision=HIGHEST):
    return lax.dot_general(a, b, dims, precision=precision, preferred_element_type=jnp.float32)


def split3(x):
    hi = x.astype(jnp.bfloat16).astype(jnp.float32)
    rest = x - hi
    mid = rest.astype(jnp.bfloat16).astype(jnp.float32)
    return hi, mid, rest - mid


def invert_factor(d_ref, w_ref):
    lane = lax.broadcasted_iota(jnp.int32, (R, B), 1)
    sub = lax.broadcasted_iota(jnp.int32, (R, B), 0)
    block_row = lax.broadcasted_iota(jnp.int32, (B, B), 0)
    block_lane = lax.broadcasted_iota(jnp.int32, (B, B), 1)

    def panel(p, carry):
        base = p * R
        rows = pl.ds(pl.multiple_of(base, R), R)
        part = d_ref[rows, :]
        front = pltpu.roll(part, lax.rem(B - base, B), 1)
        cols = [jnp.broadcast_to(front[:, j : j + 1], (R, B)) for j in range(R)]
        unit = jnp.where(lane == base + sub, 1.0, 0.0)
        scale = jnp.zeros((R, B), jnp.float32)
        for j in range(R):
            pivot = jnp.broadcast_to(cols[j][j : j + 1, :], (R, B))
            scale = jnp.where(sub == j, pivot, scale)
            if j + 1 < R:
                mult = jnp.where(sub > j, cols[j] * (1.0 / pivot), 0.0)
                for k in range(j + 1, R):
                    cols[k] = cols[k] - mult * jnp.broadcast_to(cols[k][j : j + 1, :], (R, B))
                part = part - mult * jnp.broadcast_to(part[j : j + 1, :], (R, B))
                unit = unit - mult * jnp.broadcast_to(unit[j : j + 1, :], (R, B))
        scale = lax.rsqrt(scale)
        upper = jnp.where(lane >= base + R, part * scale, 0.0)
        inverse = jnp.where(lane < base, part, unit) * scale
        w_ref[rows, :] = jnp.where(lane < base + R, inverse, 0.0)
        right = jnp.where(lane >= base + R, upper, inverse)
        ah, am, al = split3(upper)
        bh, bm, bl = split3(right)
        a = jnp.concatenate([ah, ah, am, am, ah, al], axis=0).astype(jnp.bfloat16)
        b = jnp.concatenate([bh, bm, bh, bm, bl, bh], axis=0).astype(jnp.bfloat16)
        keep = (block_row >= base + R) & (block_lane >= base) & (block_lane < base + R)
        d_ref[...] = jnp.where(keep, 0.0, d_ref[...]) - dot(a, b, TN, None)
        return carry

    lax.fori_loop(0, B // R, panel, 0)


def factor_kernel(n, gram_ref, inv_ref, d_ref, w_ref, m_ref):
    for i in range(n):
        at = B * (i * (i + 1) // 2)
        m_ref[pl.ds(i * B, B), pl.ds(0, (i + 1) * B)] = gram_ref[:, pl.ds(at, (i + 1) * B)]
    for k in range(n):
        rows = pl.ds(k * B, B)
        d_ref[...] = m_ref[rows, rows]
        invert_factor(d_ref, w_ref)
        w = w_ref[...]
        if k:
            inv_ref[rows, pl.ds(0, k * B)] = dot(w, m_ref[rows, pl.ds(0, k * B)], NN)
        inv_ref[rows, rows] = w
        if k + 1 < n:
            rest = (n - 1 - k) * B
            inv_ref[rows, pl.ds((k + 1) * B, rest)] = jnp.zeros((B, rest), jnp.float32)
            below = pl.ds((k + 1) * B, rest)
            panel = dot(m_ref[below, rows], w, NT)
            m_ref[below, rows] = -dot(panel, w, NN)
            if k:
                m_ref[below, pl.ds(0, k * B)] -= dot(panel, inv_ref[rows, pl.ds(0, k * B)], NN)
            for i in range(k + 1, n):
                a = panel[(i - k - 1) * B : (i - k) * B]
                m_ref[pl.ds(i * B, B), pl.ds((k + 1) * B, (i - k) * B)] -= dot(a, panel[: (i - k) * B], NT)


def inverse_factor(packed, width):
    n = width // B
    return pl.pallas_call(
        functools.partial(factor_kernel, n),
        out_shape=jax.ShapeDtypeStruct((width, width), jnp.float32),
        in_specs=[pl.BlockSpec(memory_space=pltpu.VMEM)],
        out_specs=pl.BlockSpec(memory_space=pltpu.VMEM),
        scratch_shapes=[
            pltpu.VMEM((B, B), jnp.float32),
            pltpu.VMEM((B, B), jnp.float32),
            pltpu.VMEM((width, width), jnp.float32),
        ],
        compiler_params=pltpu.CompilerParams(vmem_limit_bytes=32 * 1024 * 1024),
    )(packed)


def padded(shard, axis, width):
    count, length = (lax.axis_size(axis), shard.shape[0])
    up = [(i, (i + 1) % count) for i in range(count - 1)]
    down = [(j, i) for i, j in up]
    before = lax.ppermute(shard[length - width :], axis, up)
    after = lax.ppermute(shard[:width], axis, down)
    return jnp.concatenate([before, shard, after], axis=0)


def lower_blocks(rows_of, n):
    return jnp.concatenate([rows_of(i) for i in range(n)], axis=1)


def per_device(frames, conv_weight, conv_bias, proj_weight, frames_before, frames_after):
    local_frames = frames[0]
    frame_rows = local_frames.shape[0]
    width = proj_weight.shape[1]
    n = width // B
    live = (frames_before >= 0).astype(jnp.float32)
    padded_input = padded(local_frames, "tm", DILATION_STEP)
    total = jnp.zeros((frame_rows, local_frames.shape[1]), jnp.float32)
    for frame_index in range(3):
        shift_amount = (frame_index - 1) * DILATION_STEP
        valid = ((frames_before >= -shift_amount) & (frames_after >= shift_amount)).astype(
            jnp.float32
        )
        shifted_input = padded_input[
            DILATION_STEP + shift_amount : DILATION_STEP + shift_amount + frame_rows
        ]
        term = jnp.dot(shifted_input, conv_weight[frame_index], preferred_element_type=jnp.float32)
        total = total + valid[:, None] * term
    hidden = (live[:, None] * jax.nn.gelu(total + conv_bias[None, :], approximate=True)).astype(
        jnp.bfloat16
    )
    embed = jnp.dot(hidden, proj_weight, preferred_element_type=jnp.float32)

    local_count = jnp.sum(live)
    local_mean = jnp.sum(embed, axis=0) / jnp.maximum(local_count, 1.0)
    stats = lax.all_gather(
        jnp.concatenate([local_mean, jnp.broadcast_to(local_count, (B,))]), "tm"
    )
    about = live[:, None] * (embed - local_mean[None, :])
    gram = lower_blocks(
        lambda i: dot(about[:, i * B : (i + 1) * B], about[:, : (i + 1) * B], TN), n
    )
    gram = lax.psum(gram, "tm")
    counts = stats[:, width]
    means = stats[:, :width]
    count = jnp.sum(counts)
    mean = jnp.sum(counts[:, None] * means, axis=0) / count
    offset = jnp.sqrt(counts)[:, None] * (means - mean[None, :])
    between = lower_blocks(
        lambda i: dot(offset[:, i * B : (i + 1) * B], offset[:, : (i + 1) * B], TN), n
    )
    ridge = lower_blocks(lambda i: eps_shrink * jnp.eye(B, (i + 1) * B, i * B, dtype=jnp.float32), n)
    inverse = inverse_factor((gram + between) / count + ridge, width)
    centered = live[:, None] * (embed - mean[None, :])
    whitened = dot(centered, inverse, NT)

    half = frame_rows // 2
    bit = lax.axis_index("view") % 2
    pairs = [(i, i ^ 1) for i in range(lax.axis_size("view"))]
    sent = lax.dynamic_slice_in_dim(whitened, (1 - bit) * half, half).astype(jnp.bfloat16)
    partner = lax.ppermute(sent, "view", pairs).astype(jnp.float32)
    own = lax.dynamic_slice_in_dim(whitened, bit * half, half)
    diff = own - partner
    mine = jnp.sum(diff * diff, axis=1) / width
    theirs = lax.ppermute(mine, "view", pairs)
    pair_loss = jnp.where(bit == 0, jnp.concatenate([mine, theirs]), jnp.concatenate([theirs, mine]))
    return (whitened[None], pair_loss[None])


def solution(mesh):
    return jax.shard_map(
        per_device,
        mesh=mesh,
        in_specs=(P("view", "tm", None), P(), P(), P(), P("tm"), P("tm")),
        out_specs=(P("view", "tm", None), P("view", "tm")),
        check_vma=False,
    )
```

```python
import functools

import jax
import jax.numpy as jnp
from jax import lax
from jax.experimental import pallas as pl
from jax.experimental.pallas import tpu as pltpu
from jax.sharding import PartitionSpec as P

DILATION_STEP = 4
eps_shrink = 0.001
B = 128
R = 8
HIGHEST = lax.Precision.HIGHEST
NT = (((1,), (1,)), ((), ()))
NN = (((1,), (0,)), ((), ()))
TN = (((0,), (0,)), ((), ()))


def dot(a, b, dims, precision=HIGHEST):
    return lax.dot_general(a, b, dims, precision=precision, preferred_element_type=jnp.float32)


def split3(x):
    hi = x.astype(jnp.bfloat16).astype(jnp.float32)
    rest = x - hi
    mid = rest.astype(jnp.bfloat16).astype(jnp.float32)
    return hi, mid, rest - mid


def invert_factor(d_ref, w_ref):
    lane = lax.broadcasted_iota(jnp.int32, (R, B), 1)
    sub = lax.broadcasted_iota(jnp.int32, (R, B), 0)
    block_row = lax.broadcasted_iota(jnp.int32, (B, B), 0)
    block_lane = lax.broadcasted_iota(jnp.int32, (B, B), 1)

    def panel(p, carry):
        base = p * R
        rows = pl.ds(pl.multiple_of(base, R), R)
        part = d_ref[rows, :]
        front = pltpu.roll(part, lax.rem(B - base, B), 1)
        cols = [jnp.broadcast_to(front[:, j : j + 1], (R, B)) for j in range(R)]
        unit = jnp.where(lane == base + sub, 1.0, 0.0)
        scale = jnp.zeros((R, B), jnp.float32)
        for j in range(R):
            pivot = jnp.broadcast_to(cols[j][j : j + 1, :], (R, B))
            scale = jnp.where(sub == j, pivot, scale)
            if j + 1 < R:
                mult = jnp.where(sub > j, cols[j] * (1.0 / pivot), 0.0)
                for k in range(j + 1, R):
                    cols[k] = cols[k] - mult * jnp.broadcast_to(cols[k][j : j + 1, :], (R, B))
                part = part - mult * jnp.broadcast_to(part[j : j + 1, :], (R, B))
                unit = unit - mult * jnp.broadcast_to(unit[j : j + 1, :], (R, B))
        scale = lax.rsqrt(scale)
        upper = jnp.where(lane >= base + R, part * scale, 0.0)
        inverse = jnp.where(lane < base, part, unit) * scale
        w_ref[rows, :] = jnp.where(lane < base + R, inverse, 0.0)
        right = jnp.where(lane >= base + R, upper, inverse)
        ah, am, al = split3(upper)
        bh, bm, bl = split3(right)
        a = jnp.concatenate([ah, ah, am, am, ah, al], axis=0).astype(jnp.bfloat16)
        b = jnp.concatenate([bh, bm, bh, bm, bl, bh], axis=0).astype(jnp.bfloat16)
        keep = (block_row >= base + R) & (block_lane >= base) & (block_lane < base + R)
        d_ref[...] = jnp.where(keep, 0.0, d_ref[...]) - dot(a, b, TN, None)
        return carry

    lax.fori_loop(0, B // R, panel, 0)


def factor_kernel(n, gram_ref, inv_ref, d_ref, w_ref, m_ref):
    for i in range(n):
        at = B * (i * (i + 1) // 2)
        m_ref[pl.ds(i * B, B), pl.ds(0, (i + 1) * B)] = gram_ref[:, pl.ds(at, (i + 1) * B)]
    for k in range(n):
        rows = pl.ds(k * B, B)
        d_ref[...] = m_ref[rows, rows]
        invert_factor(d_ref, w_ref)
        w = w_ref[...]
        if k:
            inv_ref[rows, pl.ds(0, k * B)] = dot(w, m_ref[rows, pl.ds(0, k * B)], NN)
        inv_ref[rows, rows] = w
        if k + 1 < n:
            rest = (n - 1 - k) * B
            inv_ref[rows, pl.ds((k + 1) * B, rest)] = jnp.zeros((B, rest), jnp.float32)
            below = pl.ds((k + 1) * B, rest)
            panel = dot(m_ref[below, rows], w, NT)
            m_ref[below, rows] = -dot(panel, w, NN)
            if k:
                m_ref[below, pl.ds(0, k * B)] -= dot(panel, inv_ref[rows, pl.ds(0, k * B)], NN)
            for i in range(k + 1, n):
                a = panel[(i - k - 1) * B : (i - k) * B]
                m_ref[pl.ds(i * B, B), pl.ds((k + 1) * B, (i - k) * B)] -= dot(a, panel[: (i - k) * B], NT)


def inverse_factor(packed, width):
    n = width // B
    return pl.pallas_call(
        functools.partial(factor_kernel, n),
        out_shape=jax.ShapeDtypeStruct((width, width), jnp.float32),
        in_specs=[pl.BlockSpec(memory_space=pltpu.VMEM)],
        out_specs=pl.BlockSpec(memory_space=pltpu.VMEM),
        scratch_shapes=[
            pltpu.VMEM((B, B), jnp.float32),
            pltpu.VMEM((B, B), jnp.float32),
            pltpu.VMEM((width, width), jnp.float32),
        ],
        compiler_params=pltpu.CompilerParams(vmem_limit_bytes=32 * 1024 * 1024),
    )(packed)


def reduce_kernel(n, chunks, x_ref, stats_ref, out_ref, all_ref, half_in, half, quarter_in, quarter,
                  far_in, send_sem, recv_sem, stat_send, stat_recv):
    me = lax.axis_index("tm")
    levels = n.bit_length() - 1
    rows = x_ref.shape[0] // chunks
    h, q = rows // 2, rows // 4
    bit0, bit1 = lax.rem(me, 2), lax.rem(me // 2, 2)

    def across(level):
        size = 2**level
        return me + size * (1 - 2 * lax.rem(me // size, 2))

    barrier = pltpu.get_barrier_semaphore()
    for d in range(1, n):
        pl.semaphore_signal(
            barrier, inc=1, device_id={"tm": lax.rem(me + d, n)}, device_id_type=pl.DeviceIdType.MESH
        )
    pl.semaphore_wait(barrier, n - 1)

    def copy(src, dst, peer, ssem, rsem):
        c = pltpu.make_async_remote_copy(
            src_ref=src,
            dst_ref=dst,
            send_sem=ssem,
            recv_sem=rsem,
            device_id={"tm": peer},
            device_id_type=pl.DeviceIdType.MESH,
        )
        c.start()
        return c

    def part(start, size):
        return pl.ds(pl.multiple_of(start, q), size)

    flight = {}
    stages = levels + 2

    def step(c, stage):
        if stage:
            flight[c].wait()
        s0 = c * rows + bit0 * h
        s1 = s0 + bit1 * q
        mine = part(s1, q)
        if stage == 1:
            half[c] = x_ref[part(s0, h), :] + half_in[c]
        elif stage == 2:
            quarter[0, c] = half[c, part(bit1 * q, q), :] + quarter_in[c]
        elif 2 < stage < levels:
            quarter[stage - 2, c] = quarter[stage - 3, c] + far_in[stage - 3, c]
        elif stage == levels:
            out_ref[mine, :] = quarter[levels - 3, c] + far_in[levels - 3, c]
        if stage == stages:
            return
        if stage == 0:
            src, dst, peer = x_ref.at[part(c * rows + (1 - bit0) * h, h)], half_in.at[c], across(0)
        elif stage == 1:
            src, dst, peer = half.at[c, part((1 - bit1) * q, q)], quarter_in.at[c], across(1)
        elif stage < levels:
            src, dst, peer = quarter.at[stage - 2, c], far_in.at[stage - 2, c], across(stage)
        elif stage == levels:
            src, dst, peer = out_ref.at[mine], out_ref.at[mine], across(1)
        else:
            own = part(s0, h)
            src, dst, peer = out_ref.at[own], out_ref.at[own], across(0)
        flight[c] = copy(src, dst, peer, send_sem.at[stage, c], recv_sem.at[stage, c])

    for c in range(chunks):
        step(c, 0)
    all_ref[me] = stats_ref[...]
    gathers = [
        copy(stats_ref, all_ref.at[me], lax.rem(me + d, n), stat_send.at[d], stat_recv.at[d])
        for d in range(1, n)
    ]
    for t in range(1, chunks + stages):
        for c in range(chunks):
            if 1 <= t - c <= stages:
                step(c, t - c)
    for g in gathers:
        g.wait()


def reduce_and_gather(packed, stats, n):
    assert n >= 8 and n & (n - 1) == 0
    chunks = 4
    levels = n.bit_length() - 1
    height, width = packed.shape
    h, q = height // chunks // 2, height // chunks // 4
    f32 = jnp.float32
    vmem = pl.BlockSpec(memory_space=pltpu.VMEM)
    return pl.pallas_call(
        functools.partial(reduce_kernel, n, chunks),
        out_shape=(
            jax.ShapeDtypeStruct((height, width), f32),
            jax.ShapeDtypeStruct((n,) + stats.shape, f32),
        ),
        in_specs=[vmem] * 2,
        out_specs=(vmem, vmem),
        scratch_shapes=[
            pltpu.VMEM((chunks, h, width), f32),
            pltpu.VMEM((chunks, h, width), f32),
            pltpu.VMEM((chunks, q, width), f32),
            pltpu.VMEM((levels - 2, chunks, q, width), f32),
            pltpu.VMEM((levels - 2, chunks, q, width), f32),
            pltpu.SemaphoreType.DMA((levels + 2, chunks)),
            pltpu.SemaphoreType.DMA((levels + 2, chunks)),
            pltpu.SemaphoreType.DMA((n,)),
            pltpu.SemaphoreType.DMA((n,)),
        ],
        compiler_params=pltpu.CompilerParams(
            collective_id=0, has_side_effects=True, vmem_limit_bytes=32 * 1024 * 1024
        ),
    )(packed, stats)


def padded(shard, axis, width):
    count, length = (lax.axis_size(axis), shard.shape[0])
    up = [(i, (i + 1) % count) for i in range(count - 1)]
    down = [(j, i) for i, j in up]
    before = lax.ppermute(shard[length - width :], axis, up)
    after = lax.ppermute(shard[:width], axis, down)
    return jnp.concatenate([before, shard, after], axis=0)


def lower_blocks(rows_of, n):
    return jnp.concatenate([rows_of(i) for i in range(n)], axis=1)


def per_device(frames, conv_weight, conv_bias, proj_weight, frames_before, frames_after):
    local_frames = frames[0]
    frame_rows = local_frames.shape[0]
    width = proj_weight.shape[1]
    n = width // B
    live = (frames_before >= 0).astype(jnp.float32)
    padded_input = padded(local_frames, "tm", DILATION_STEP)
    total = jnp.zeros((frame_rows, local_frames.shape[1]), jnp.float32)
    for frame_index in range(3):
        shift_amount = (frame_index - 1) * DILATION_STEP
        valid = ((frames_before >= -shift_amount) & (frames_after >= shift_amount)).astype(
            jnp.float32
        )
        shifted_input = padded_input[
            DILATION_STEP + shift_amount : DILATION_STEP + shift_amount + frame_rows
        ]
        term = jnp.dot(shifted_input, conv_weight[frame_index], preferred_element_type=jnp.float32)
        total = total + valid[:, None] * term
    hidden = (live[:, None] * jax.nn.gelu(total + conv_bias[None, :], approximate=True)).astype(
        jnp.bfloat16
    )
    embed = jnp.dot(hidden, proj_weight, preferred_element_type=jnp.float32)

    local_count = jnp.sum(live)
    local_mean = jnp.sum(embed, axis=0) / jnp.maximum(local_count, 1.0)
    stats = jnp.concatenate([local_mean, jnp.broadcast_to(local_count, (B,))])[None]
    about = live[:, None] * (embed - local_mean[None, :])
    pair = 2 * B
    bands = [
        dot(about[:, i * pair : (i + 1) * pair], about[:, : (i + 1) * pair], TN) for i in range(n // 2)
    ]
    gram = lower_blocks(
        lambda i: bands[i // 2][(i % 2) * B : (i % 2 + 1) * B, : (i + 1) * B], n
    )
    gram, stats = reduce_and_gather(gram, stats, lax.axis_size("tm"))
    stats = stats[:, 0]
    counts = stats[:, width]
    means = stats[:, :width]
    count = jnp.sum(counts)
    mean = jnp.sum(counts[:, None] * means, axis=0) / count
    offset = jnp.sqrt(counts)[:, None] * (means - mean[None, :])
    between = lower_blocks(
        lambda i: dot(offset[:, i * B : (i + 1) * B], offset[:, : (i + 1) * B], TN), n
    )
    ridge = lower_blocks(lambda i: eps_shrink * jnp.eye(B, (i + 1) * B, i * B, dtype=jnp.float32), n)
    inverse = inverse_factor((gram + between) / count + ridge, width)
    centered = live[:, None] * (embed - mean[None, :])
    whitened = dot(centered, inverse, NT)

    half = frame_rows // 2
    bit = lax.axis_index("view") % 2
    pairs = [(i, i ^ 1) for i in range(lax.axis_size("view"))]
    sent = lax.dynamic_slice_in_dim(whitened, (1 - bit) * half, half).astype(jnp.bfloat16)
    partner = lax.ppermute(sent, "view", pairs).astype(jnp.float32)
    own = lax.dynamic_slice_in_dim(whitened, bit * half, half)
    diff = own - partner
    mine = jnp.sum(diff * diff, axis=1) / width
    theirs = lax.ppermute(mine, "view", pairs)
    pair_loss = jnp.where(bit == 0, jnp.concatenate([mine, theirs]), jnp.concatenate([theirs, mine]))
    return (whitened[None], pair_loss[None])


def solution(mesh):
    return jax.shard_map(
        per_device,
        mesh=mesh,
        in_specs=(P("view", "tm", None), P(), P(), P(), P("tm"), P("tm")),
        out_specs=(P("view", "tm", None), P("view", "tm")),
        check_vma=False,
    )
```

```python
import functools

import jax
import jax.numpy as jnp
from jax import lax
from jax.experimental import pallas as pl
from jax.experimental.pallas import tpu as pltpu
from jax.sharding import PartitionSpec as P

DILATION_STEP = 4
eps_shrink = 0.001
B = 128
R = 8
HIGHEST = lax.Precision.HIGHEST
NT = (((1,), (1,)), ((), ()))
NN = (((1,), (0,)), ((), ()))
TN = (((0,), (0,)), ((), ()))


def dot(a, b, dims, precision=HIGHEST):
    return lax.dot_general(a, b, dims, precision=precision, preferred_element_type=jnp.float32)


def split3(x):
    hi = x.astype(jnp.bfloat16).astype(jnp.float32)
    rest = x - hi
    mid = rest.astype(jnp.bfloat16).astype(jnp.float32)
    return hi, mid, rest - mid


def invert_factor(d_ref, w_ref):
    lane = lax.broadcasted_iota(jnp.int32, (R, B), 1)
    sub = lax.broadcasted_iota(jnp.int32, (R, B), 0)
    block_row = lax.broadcasted_iota(jnp.int32, (B, B), 0)
    block_lane = lax.broadcasted_iota(jnp.int32, (B, B), 1)

    def panel(p, carry):
        base = p * R
        rows = pl.ds(pl.multiple_of(base, R), R)
        part = d_ref[rows, :]
        front = pltpu.roll(part, lax.rem(B - base, B), 1)
        cols = [jnp.broadcast_to(front[:, j : j + 1], (R, B)) for j in range(R)]
        unit = jnp.where(lane == base + sub, 1.0, 0.0)
        scale = jnp.zeros((R, B), jnp.float32)
        for j in range(R):
            pivot = jnp.broadcast_to(cols[j][j : j + 1, :], (R, B))
            scale = jnp.where(sub == j, pivot, scale)
            if j + 1 < R:
                mult = jnp.where(sub > j, cols[j] * (1.0 / pivot), 0.0)
                for k in range(j + 1, R):
                    cols[k] = cols[k] - mult * jnp.broadcast_to(cols[k][j : j + 1, :], (R, B))
                part = part - mult * jnp.broadcast_to(part[j : j + 1, :], (R, B))
                unit = unit - mult * jnp.broadcast_to(unit[j : j + 1, :], (R, B))
        scale = lax.rsqrt(scale)
        upper = jnp.where(lane >= base + R, part * scale, 0.0)
        inverse = jnp.where(lane < base, part, unit) * scale
        w_ref[rows, :] = jnp.where(lane < base + R, inverse, 0.0)
        right = jnp.where(lane >= base + R, upper, inverse)
        ah, am, al = split3(upper)
        bh, bm, bl = split3(right)
        a = jnp.concatenate([ah, ah, am, am, ah, al], axis=0).astype(jnp.bfloat16)
        b = jnp.concatenate([bh, bm, bh, bm, bl, bh], axis=0).astype(jnp.bfloat16)
        keep = (block_row >= base + R) & (block_lane >= base) & (block_lane < base + R)
        d_ref[...] = jnp.where(keep, 0.0, d_ref[...]) - dot(a, b, TN, None)
        return carry

    lax.fori_loop(0, B // R, panel, 0)


def factor_kernel(n, gram_ref, inv_ref, d_ref, w_ref, m_ref):
    for i in range(n):
        at = B * (i * (i + 1) // 2)
        m_ref[pl.ds(i * B, B), pl.ds(0, (i + 1) * B)] = gram_ref[:, pl.ds(at, (i + 1) * B)]
    for k in range(n):
        rows = pl.ds(k * B, B)
        d_ref[...] = m_ref[rows, rows]
        invert_factor(d_ref, w_ref)
        w = w_ref[...]
        if k:
            inv_ref[rows, pl.ds(0, k * B)] = dot(w, m_ref[rows, pl.ds(0, k * B)], NN)
        inv_ref[rows, rows] = w
        if k + 1 < n:
            rest = (n - 1 - k) * B
            inv_ref[rows, pl.ds((k + 1) * B, rest)] = jnp.zeros((B, rest), jnp.float32)
            below = pl.ds((k + 1) * B, rest)
            panel = dot(m_ref[below, rows], w, NT)
            m_ref[below, rows] = -dot(panel, w, NN)
            if k:
                m_ref[below, pl.ds(0, k * B)] -= dot(panel, inv_ref[rows, pl.ds(0, k * B)], NN)
            for i in range(k + 1, n):
                a = panel[(i - k - 1) * B : (i - k) * B]
                m_ref[pl.ds(i * B, B), pl.ds((k + 1) * B, (i - k) * B)] -= dot(a, panel[: (i - k) * B], NT)


def inverse_factor(packed, width):
    n = width // B
    return pl.pallas_call(
        functools.partial(factor_kernel, n),
        out_shape=jax.ShapeDtypeStruct((width, width), jnp.float32),
        in_specs=[pl.BlockSpec(memory_space=pltpu.VMEM)],
        out_specs=pl.BlockSpec(memory_space=pltpu.VMEM),
        scratch_shapes=[
            pltpu.VMEM((B, B), jnp.float32),
            pltpu.VMEM((B, B), jnp.float32),
            pltpu.VMEM((width, width), jnp.float32),
        ],
        compiler_params=pltpu.CompilerParams(vmem_limit_bytes=32 * 1024 * 1024),
    )(packed)


def reduce_kernel(n, chunks, x_ref, stats_ref, out_ref, all_ref, half_in, half, quarter_in, quarter,
                  far_in, send_sem, recv_sem, stat_send, stat_recv):
    me = lax.axis_index("tm")
    levels = n.bit_length() - 1
    rows = x_ref.shape[0] // chunks
    h, q = rows // 2, rows // 4
    bit0, bit1 = lax.rem(me, 2), lax.rem(me // 2, 2)

    def across(level):
        size = 2**level
        return me + size * (1 - 2 * lax.rem(me // size, 2))

    barrier = pltpu.get_barrier_semaphore()
    for d in range(1, n):
        pl.semaphore_signal(
            barrier, inc=1, device_id={"tm": lax.rem(me + d, n)}, device_id_type=pl.DeviceIdType.MESH
        )
    pl.semaphore_wait(barrier, n - 1)

    def copy(src, dst, peer, ssem, rsem):
        c = pltpu.make_async_remote_copy(
            src_ref=src,
            dst_ref=dst,
            send_sem=ssem,
            recv_sem=rsem,
            device_id={"tm": peer},
            device_id_type=pl.DeviceIdType.MESH,
        )
        c.start()
        return c

    def part(start, size):
        return pl.ds(pl.multiple_of(start, q), size)

    flight = {}
    stages = levels + 2

    def step(c, stage):
        if stage:
            flight[c].wait()
        s0 = c * rows + bit0 * h
        s1 = s0 + bit1 * q
        mine = part(s1, q)
        if stage == 1:
            half[c] = x_ref[part(s0, h), :] + half_in[c]
        elif stage == 2:
            quarter[0, c] = half[c, part(bit1 * q, q), :] + quarter_in[c]
        elif 2 < stage < levels:
            quarter[stage - 2, c] = quarter[stage - 3, c] + far_in[stage - 3, c]
        elif stage == levels:
            out_ref[mine, :] = quarter[levels - 3, c] + far_in[levels - 3, c]
        if stage == stages:
            return
        if stage == 0:
            src, dst, peer = x_ref.at[part(c * rows + (1 - bit0) * h, h)], half_in.at[c], across(0)
        elif stage == 1:
            src, dst, peer = half.at[c, part((1 - bit1) * q, q)], quarter_in.at[c], across(1)
        elif stage < levels:
            src, dst, peer = quarter.at[stage - 2, c], far_in.at[stage - 2, c], across(stage)
        elif stage == levels:
            src, dst, peer = out_ref.at[mine], out_ref.at[mine], across(1)
        else:
            own = part(s0, h)
            src, dst, peer = out_ref.at[own], out_ref.at[own], across(0)
        flight[c] = copy(src, dst, peer, send_sem.at[stage, c], recv_sem.at[stage, c])

    for c in range(chunks):
        step(c, 0)
    all_ref[me] = stats_ref[...]
    gathers = [
        copy(stats_ref, all_ref.at[me], lax.rem(me + d, n), stat_send.at[d], stat_recv.at[d])
        for d in range(1, n)
    ]
    for t in range(1, chunks + stages):
        for c in range(chunks):
            if 1 <= t - c <= stages:
                step(c, t - c)
    for g in gathers:
        g.wait()


def reduce_and_gather(packed, stats, n):
    assert n >= 8 and n & (n - 1) == 0
    chunks = 4
    levels = n.bit_length() - 1
    height, width = packed.shape
    h, q = height // chunks // 2, height // chunks // 4
    f32 = jnp.float32
    vmem = pl.BlockSpec(memory_space=pltpu.VMEM)
    return pl.pallas_call(
        functools.partial(reduce_kernel, n, chunks),
        out_shape=(
            jax.ShapeDtypeStruct((height, width), f32),
            jax.ShapeDtypeStruct((n,) + stats.shape, f32),
        ),
        in_specs=[vmem] * 2,
        out_specs=(vmem, vmem),
        scratch_shapes=[
            pltpu.VMEM((chunks, h, width), f32),
            pltpu.VMEM((chunks, h, width), f32),
            pltpu.VMEM((chunks, q, width), f32),
            pltpu.VMEM((levels - 2, chunks, q, width), f32),
            pltpu.VMEM((levels - 2, chunks, q, width), f32),
            pltpu.SemaphoreType.DMA((levels + 2, chunks)),
            pltpu.SemaphoreType.DMA((levels + 2, chunks)),
            pltpu.SemaphoreType.DMA((n,)),
            pltpu.SemaphoreType.DMA((n,)),
        ],
        compiler_params=pltpu.CompilerParams(
            collective_id=0, has_side_effects=True, vmem_limit_bytes=32 * 1024 * 1024
        ),
    )(packed, stats)


def padded(shard, axis, width):
    count, length = (lax.axis_size(axis), shard.shape[0])
    up = [(i, (i + 1) % count) for i in range(count - 1)]
    down = [(j, i) for i, j in up]
    before = lax.ppermute(shard[length - width :], axis, up)
    after = lax.ppermute(shard[:width], axis, down)
    return jnp.concatenate([before, shard, after], axis=0)


def lower_blocks(rows_of, n):
    return jnp.concatenate([rows_of(i) for i in range(n)], axis=1)


def per_device(frames, conv_weight, conv_bias, proj_weight, frames_before, frames_after):
    local_frames = frames[0]
    frame_rows = local_frames.shape[0]
    width = proj_weight.shape[1]
    n = width // B
    live = (frames_before >= 0).astype(jnp.float32)
    padded_input = padded(local_frames, "tm", DILATION_STEP)
    total = jnp.zeros((frame_rows, local_frames.shape[1]), jnp.float32)
    for frame_index in range(3):
        shift_amount = (frame_index - 1) * DILATION_STEP
        valid = ((frames_before >= -shift_amount) & (frames_after >= shift_amount)).astype(
            jnp.float32
        )
        shifted_input = padded_input[
            DILATION_STEP + shift_amount : DILATION_STEP + shift_amount + frame_rows
        ]
        term = jnp.dot(shifted_input, conv_weight[frame_index], preferred_element_type=jnp.float32)
        total = total + valid[:, None] * term
    hidden = (live[:, None] * jax.nn.gelu(total + conv_bias[None, :], approximate=True)).astype(
        jnp.bfloat16
    )
    embed = jnp.dot(hidden, proj_weight, preferred_element_type=jnp.float32)

    local_count = jnp.sum(live)
    local_mean = jnp.sum(embed, axis=0) / jnp.maximum(local_count, 1.0)
    stats = jnp.concatenate([local_mean, jnp.broadcast_to(local_count, (B,))])[None]
    about = live[:, None] * (embed - local_mean[None, :])
    pair = 2 * B
    bands = [
        dot(about[:, i * pair : (i + 1) * pair], about[:, : (i + 1) * pair], TN) for i in range(n // 2)
    ]
    gram = lower_blocks(
        lambda i: bands[i // 2][(i % 2) * B : (i % 2 + 1) * B, : (i + 1) * B], n
    )
    gram, stats = reduce_and_gather(gram, stats, lax.axis_size("tm"))
    stats = stats[:, 0]
    counts = stats[:, width]
    means = stats[:, :width]
    count = jnp.sum(counts)
    mean = jnp.sum(counts[:, None] * means, axis=0) / count
    offset = jnp.sqrt(counts)[:, None] * (means - mean[None, :])
    between = lower_blocks(
        lambda i: dot(offset[:, i * B : (i + 1) * B], offset[:, : (i + 1) * B], TN), n
    )
    ridge = lower_blocks(lambda i: eps_shrink * jnp.eye(B, (i + 1) * B, i * B, dtype=jnp.float32), n)
    inverse = inverse_factor((gram + between) / count + ridge, width)

    def whiten(start, size):
        rows = lax.dynamic_slice_in_dim(embed, start, size)
        here = lax.dynamic_slice_in_dim(live, start, size)
        return dot(here[:, None] * (rows - mean[None, :]), inverse, NT)

    half = frame_rows // 2
    piece = half // 2
    bit = lax.axis_index("view") % 2
    pairs = [(i, i ^ 1) for i in range(lax.axis_size("view"))]
    whitened = jnp.zeros((frame_rows, width), jnp.float32)
    arrived = []
    for k in range(2):
        start = (1 - bit) * half + k * piece
        first = whiten(start, piece)
        arrived.append(lax.ppermute(first.astype(jnp.bfloat16), "view", pairs))
        whitened = lax.dynamic_update_slice_in_dim(whitened, first, start, 0)
    own = whiten(bit * half, half)
    whitened = lax.dynamic_update_slice_in_dim(whitened, own, bit * half, 0)
    losses = []
    for k in range(2):
        diff = own[k * piece : (k + 1) * piece] - arrived[k].astype(jnp.float32)
        losses.append(jnp.sum(diff * diff, axis=1) / width)
    mine = jnp.concatenate(losses)
    theirs = lax.ppermute(mine, "view", pairs)
    pair_loss = jnp.where(bit == 0, jnp.concatenate([mine, theirs]), jnp.concatenate([theirs, mine]))
    return (whitened[None], pair_loss[None])


def solution(mesh):
    return jax.shard_map(
        per_device,
        mesh=mesh,
        in_specs=(P("view", "tm", None), P(), P(), P(), P("tm"), P("tm")),
        out_specs=(P("view", "tm", None), P("view", "tm")),
        check_vma=False,
    )
```

```python
import functools

import jax
import jax.numpy as jnp
from jax import lax
from jax.experimental import pallas as pl
from jax.experimental.pallas import tpu as pltpu
from jax.sharding import PartitionSpec as P

DILATION_STEP = 4
eps_shrink = 0.001
B = 128
R = 16
HIGHEST = lax.Precision.HIGHEST
NT = (((1,), (1,)), ((), ()))
NN = (((1,), (0,)), ((), ()))
TN = (((0,), (0,)), ((), ()))


def dot(a, b, dims, precision=HIGHEST):
    return lax.dot_general(a, b, dims, precision=precision, preferred_element_type=jnp.float32)


def split3(x):
    hi = x.astype(jnp.bfloat16).astype(jnp.float32)
    rest = x - hi
    mid = rest.astype(jnp.bfloat16).astype(jnp.float32)
    return hi, mid, rest - mid


def invert_factor(d_ref, w_ref):
    lane = lax.broadcasted_iota(jnp.int32, (R, B), 1)
    sub = lax.broadcasted_iota(jnp.int32, (R, B), 0)
    block_row = lax.broadcasted_iota(jnp.int32, (B, B), 0)
    block_lane = lax.broadcasted_iota(jnp.int32, (B, B), 1)

    def panel(p, carry):
        base = p * R
        rows = pl.ds(pl.multiple_of(base, R), R)
        part = d_ref[rows, :]
        front = pltpu.roll(part, lax.rem(B - base, B), 1)
        cols = [jnp.broadcast_to(front[:, j : j + 1], (R, B)) for j in range(R)]
        unit = jnp.where(lane == base + sub, 1.0, 0.0)
        scale = jnp.zeros((R, B), jnp.float32)
        for j in range(R):
            pivot = jnp.broadcast_to(cols[j][j : j + 1, :], (R, B))
            scale = jnp.where(sub == j, pivot, scale)
            if j + 1 < R:
                mult = jnp.where(sub > j, cols[j] * (1.0 / pivot), 0.0)
                for k in range(j + 1, R):
                    cols[k] = cols[k] - mult * jnp.broadcast_to(cols[k][j : j + 1, :], (R, B))
                part = part - mult * jnp.broadcast_to(part[j : j + 1, :], (R, B))
                unit = unit - mult * jnp.broadcast_to(unit[j : j + 1, :], (R, B))
        scale = lax.rsqrt(scale)
        upper = jnp.where(lane >= base + R, part * scale, 0.0)
        inverse = jnp.where(lane < base, part, unit) * scale
        w_ref[rows, :] = jnp.where(lane < base + R, inverse, 0.0)
        right = jnp.where(lane >= base + R, upper, inverse)
        ah, am, al = split3(upper)
        bh, bm, bl = split3(right)
        a = jnp.concatenate([ah, ah, am, am, ah, al], axis=0).astype(jnp.bfloat16)
        b = jnp.concatenate([bh, bm, bh, bm, bl, bh], axis=0).astype(jnp.bfloat16)
        keep = (block_row >= base + R) & (block_lane >= base) & (block_lane < base + R)
        d_ref[...] = jnp.where(keep, 0.0, d_ref[...]) - dot(a, b, TN, None)
        return carry

    lax.fori_loop(0, B // R, panel, 0)


def factor_kernel(n, gram_ref, inv_ref, d_ref, w_ref, m_ref):
    for i in range(n):
        at = B * (i * (i + 1) // 2)
        m_ref[pl.ds(i * B, B), pl.ds(0, (i + 1) * B)] = gram_ref[:, pl.ds(at, (i + 1) * B)]
    for k in range(n):
        rows = pl.ds(k * B, B)
        d_ref[...] = m_ref[rows, rows]
        invert_factor(d_ref, w_ref)
        w = w_ref[...]
        if k:
            inv_ref[rows, pl.ds(0, k * B)] = dot(w, m_ref[rows, pl.ds(0, k * B)], NN)
        inv_ref[rows, rows] = w
        if k + 1 < n:
            rest = (n - 1 - k) * B
            inv_ref[rows, pl.ds((k + 1) * B, rest)] = jnp.zeros((B, rest), jnp.float32)
            below = pl.ds((k + 1) * B, rest)
            panel = dot(m_ref[below, rows], w, NT)
            m_ref[below, rows] = -dot(panel, w, NN)
            if k:
                m_ref[below, pl.ds(0, k * B)] -= dot(panel, inv_ref[rows, pl.ds(0, k * B)], NN)
            for i in range(k + 1, n):
                a = panel[(i - k - 1) * B : (i - k) * B]
                m_ref[pl.ds(i * B, B), pl.ds((k + 1) * B, (i - k) * B)] -= dot(a, panel[: (i - k) * B], NT)


def inverse_factor(packed, width):
    n = width // B
    return pl.pallas_call(
        functools.partial(factor_kernel, n),
        out_shape=jax.ShapeDtypeStruct((width, width), jnp.float32),
        in_specs=[pl.BlockSpec(memory_space=pltpu.VMEM)],
        out_specs=pl.BlockSpec(memory_space=pltpu.VMEM),
        scratch_shapes=[
            pltpu.VMEM((B, B), jnp.float32),
            pltpu.VMEM((B, B), jnp.float32),
            pltpu.VMEM((width, width), jnp.float32),
        ],
        compiler_params=pltpu.CompilerParams(vmem_limit_bytes=32 * 1024 * 1024),
    )(packed)


def reduce_kernel(n, chunks, x_ref, stats_ref, out_ref, all_ref, half_in, half, quarter_in, quarter,
                  far_in, send_sem, recv_sem, stat_send, stat_recv):
    me = lax.axis_index("tm")
    levels = n.bit_length() - 1
    rows = x_ref.shape[0] // chunks
    h, q = rows // 2, rows // 4
    bit0, bit1 = lax.rem(me, 2), lax.rem(me // 2, 2)

    def across(level):
        size = 2**level
        return me + size * (1 - 2 * lax.rem(me // size, 2))

    barrier = pltpu.get_barrier_semaphore()
    for d in range(1, n):
        pl.semaphore_signal(
            barrier, inc=1, device_id={"tm": lax.rem(me + d, n)}, device_id_type=pl.DeviceIdType.MESH
        )
    pl.semaphore_wait(barrier, n - 1)

    def copy(src, dst, peer, ssem, rsem):
        c = pltpu.make_async_remote_copy(
            src_ref=src,
            dst_ref=dst,
            send_sem=ssem,
            recv_sem=rsem,
            device_id={"tm": peer},
            device_id_type=pl.DeviceIdType.MESH,
        )
        c.start()
        return c

    def part(start, size):
        return pl.ds(pl.multiple_of(start, q), size)

    flight = {}
    stages = levels + 2

    def step(c, stage):
        if stage:
            flight[c].wait()
        s0 = c * rows + bit0 * h
        s1 = s0 + bit1 * q
        mine = part(s1, q)
        if stage == 1:
            half[c] = x_ref[part(s0, h), :] + half_in[c]
        elif stage == 2:
            quarter[0, c] = half[c, part(bit1 * q, q), :] + quarter_in[c]
        elif 2 < stage < levels:
            quarter[stage - 2, c] = quarter[stage - 3, c] + far_in[stage - 3, c]
        elif stage == levels:
            out_ref[mine, :] = quarter[levels - 3, c] + far_in[levels - 3, c]
        if stage == stages:
            return
        if stage == 0:
            src, dst, peer = x_ref.at[part(c * rows + (1 - bit0) * h, h)], half_in.at[c], across(0)
        elif stage == 1:
            src, dst, peer = half.at[c, part((1 - bit1) * q, q)], quarter_in.at[c], across(1)
        elif stage < levels:
            src, dst, peer = quarter.at[stage - 2, c], far_in.at[stage - 2, c], across(stage)
        elif stage == levels:
            src, dst, peer = out_ref.at[mine], out_ref.at[mine], across(1)
        else:
            own = part(s0, h)
            src, dst, peer = out_ref.at[own], out_ref.at[own], across(0)
        flight[c] = copy(src, dst, peer, send_sem.at[stage, c], recv_sem.at[stage, c])

    for c in range(chunks):
        step(c, 0)
    all_ref[me] = stats_ref[...]
    gathers = [
        copy(stats_ref, all_ref.at[me], lax.rem(me + d, n), stat_send.at[d], stat_recv.at[d])
        for d in range(1, n)
    ]
    for t in range(1, chunks + stages):
        for c in range(chunks):
            if 1 <= t - c <= stages:
                step(c, t - c)
    for g in gathers:
        g.wait()


def reduce_and_gather(packed, stats, n):
    assert n >= 8 and n & (n - 1) == 0
    chunks = 4
    levels = n.bit_length() - 1
    height, width = packed.shape
    h, q = height // chunks // 2, height // chunks // 4
    f32 = jnp.float32
    vmem = pl.BlockSpec(memory_space=pltpu.VMEM)
    return pl.pallas_call(
        functools.partial(reduce_kernel, n, chunks),
        out_shape=(
            jax.ShapeDtypeStruct((height, width), f32),
            jax.ShapeDtypeStruct((n,) + stats.shape, f32),
        ),
        in_specs=[vmem] * 2,
        out_specs=(vmem, vmem),
        scratch_shapes=[
            pltpu.VMEM((chunks, h, width), f32),
            pltpu.VMEM((chunks, h, width), f32),
            pltpu.VMEM((chunks, q, width), f32),
            pltpu.VMEM((levels - 2, chunks, q, width), f32),
            pltpu.VMEM((levels - 2, chunks, q, width), f32),
            pltpu.SemaphoreType.DMA((levels + 2, chunks)),
            pltpu.SemaphoreType.DMA((levels + 2, chunks)),
            pltpu.SemaphoreType.DMA((n,)),
            pltpu.SemaphoreType.DMA((n,)),
        ],
        compiler_params=pltpu.CompilerParams(
            collective_id=0, has_side_effects=True, vmem_limit_bytes=32 * 1024 * 1024
        ),
    )(packed, stats)


def padded(shard, axis, width):
    count, length = (lax.axis_size(axis), shard.shape[0])
    up = [(i, (i + 1) % count) for i in range(count - 1)]
    down = [(j, i) for i, j in up]
    before = lax.ppermute(shard[length - width :], axis, up)
    after = lax.ppermute(shard[:width], axis, down)
    return jnp.concatenate([before, shard, after], axis=0)


def lower_blocks(rows_of, n):
    return jnp.concatenate([rows_of(i) for i in range(n)], axis=1)


def per_device(frames, conv_weight, conv_bias, proj_weight, frames_before, frames_after):
    local_frames = frames[0]
    frame_rows = local_frames.shape[0]
    width = proj_weight.shape[1]
    n = width // B
    live = (frames_before >= 0).astype(jnp.float32)
    padded_input = padded(local_frames, "tm", DILATION_STEP)
    total = jnp.zeros((frame_rows, local_frames.shape[1]), jnp.float32)
    for frame_index in range(3):
        shift_amount = (frame_index - 1) * DILATION_STEP
        valid = ((frames_before >= -shift_amount) & (frames_after >= shift_amount)).astype(
            jnp.float32
        )
        shifted_input = padded_input[
            DILATION_STEP + shift_amount : DILATION_STEP + shift_amount + frame_rows
        ]
        term = jnp.dot(shifted_input, conv_weight[frame_index], preferred_element_type=jnp.float32)
        total = total + valid[:, None] * term
    hidden = (live[:, None] * jax.nn.gelu(total + conv_bias[None, :], approximate=True)).astype(
        jnp.bfloat16
    )
    embed = jnp.dot(hidden, proj_weight, preferred_element_type=jnp.float32)

    local_count = jnp.sum(live)
    local_mean = jnp.sum(embed, axis=0) / jnp.maximum(local_count, 1.0)
    stats = jnp.concatenate([local_mean, jnp.broadcast_to(local_count, (B,))])[None]
    about = live[:, None] * (embed - local_mean[None, :])
    pair = 2 * B
    bands = [
        dot(about[:, i * pair : (i + 1) * pair], about[:, : (i + 1) * pair], TN) for i in range(n // 2)
    ]
    gram = lower_blocks(
        lambda i: bands[i // 2][(i % 2) * B : (i % 2 + 1) * B, : (i + 1) * B], n
    )
    gram, stats = reduce_and_gather(gram, stats, lax.axis_size("tm"))
    stats = stats[:, 0]
    counts = stats[:, width]
    means = stats[:, :width]
    count = jnp.sum(counts)
    mean = jnp.sum(counts[:, None] * means, axis=0) / count
    offset = jnp.sqrt(counts)[:, None] * (means - mean[None, :])
    between = lower_blocks(
        lambda i: dot(offset[:, i * B : (i + 1) * B], offset[:, : (i + 1) * B], TN), n
    )
    ridge = lower_blocks(lambda i: eps_shrink * jnp.eye(B, (i + 1) * B, i * B, dtype=jnp.float32), n)
    inverse = inverse_factor((gram + between) / count + ridge, width)

    def whiten(start, size):
        rows = lax.dynamic_slice_in_dim(embed, start, size)
        here = lax.dynamic_slice_in_dim(live, start, size)
        return dot(here[:, None] * (rows - mean[None, :]), inverse, NT)

    half = frame_rows // 2
    piece = half // 2
    bit = lax.axis_index("view") % 2
    pairs = [(i, i ^ 1) for i in range(lax.axis_size("view"))]
    whitened = jnp.zeros((frame_rows, width), jnp.float32)
    arrived = []
    for k in range(2):
        start = (1 - bit) * half + k * piece
        first = whiten(start, piece)
        arrived.append(lax.ppermute(first.astype(jnp.bfloat16), "view", pairs))
        whitened = lax.dynamic_update_slice_in_dim(whitened, first, start, 0)
    own = whiten(bit * half, half)
    whitened = lax.dynamic_update_slice_in_dim(whitened, own, bit * half, 0)
    losses = []
    for k in range(2):
        diff = own[k * piece : (k + 1) * piece] - arrived[k].astype(jnp.float32)
        losses.append(jnp.sum(diff * diff, axis=1) / width)
    mine = jnp.concatenate(losses)
    theirs = lax.ppermute(mine, "view", pairs)
    pair_loss = jnp.where(bit == 0, jnp.concatenate([mine, theirs]), jnp.concatenate([theirs, mine]))
    return (whitened[None], pair_loss[None])


def solution(mesh):
    return jax.shard_map(
        per_device,
        mesh=mesh,
        in_specs=(P("view", "tm", None), P(), P(), P(), P("tm"), P("tm")),
        out_specs=(P("view", "tm", None), P("view", "tm")),
        check_vma=False,
    )
```

```python
import functools

import jax
import jax.numpy as jnp
from jax import lax
from jax.experimental import pallas as pl
from jax.experimental.pallas import tpu as pltpu
from jax.sharding import PartitionSpec as P

DILATION_STEP = 4
eps_shrink = 0.001
B = 128
R = 16
HIGHEST = lax.Precision.HIGHEST
NT = (((1,), (1,)), ((), ()))
NN = (((1,), (0,)), ((), ()))
TN = (((0,), (0,)), ((), ()))


def dot(a, b, dims, precision=HIGHEST):
    return lax.dot_general(a, b, dims, precision=precision, preferred_element_type=jnp.float32)


def split3(x):
    hi = x.astype(jnp.bfloat16).astype(jnp.float32)
    rest = x - hi
    mid = rest.astype(jnp.bfloat16).astype(jnp.float32)
    return hi, mid, rest - mid


def invert_factor(d_ref, w_ref):
    lane = lax.broadcasted_iota(jnp.int32, (R, B), 1)
    sub = lax.broadcasted_iota(jnp.int32, (R, B), 0)
    block_row = lax.broadcasted_iota(jnp.int32, (B, B), 0)
    block_lane = lax.broadcasted_iota(jnp.int32, (B, B), 1)

    def panel(p, carry):
        base = p * R
        rows = pl.ds(pl.multiple_of(base, R), R)
        part = d_ref[rows, :]
        front = pltpu.roll(part, lax.rem(B - base, B), 1)
        cols = [jnp.broadcast_to(front[:, j : j + 1], (R, B)) for j in range(R)]
        unit = jnp.where(lane == base + sub, 1.0, 0.0)
        scale = jnp.zeros((R, B), jnp.float32)
        for j in range(R):
            pivot = jnp.broadcast_to(cols[j][j : j + 1, :], (R, B))
            scale = jnp.where(sub == j, pivot, scale)
            if j + 1 < R:
                mult = jnp.where(sub > j, cols[j] * (1.0 / pivot), 0.0)
                for k in range(j + 1, R):
                    cols[k] = cols[k] - mult * jnp.broadcast_to(cols[k][j : j + 1, :], (R, B))
                part = part - mult * jnp.broadcast_to(part[j : j + 1, :], (R, B))
                unit = unit - mult * jnp.broadcast_to(unit[j : j + 1, :], (R, B))
        scale = lax.rsqrt(scale)
        upper = jnp.where(lane >= base + R, part * scale, 0.0)
        inverse = jnp.where(lane < base, part, unit) * scale
        w_ref[rows, :] = jnp.where(lane < base + R, inverse, 0.0)
        right = jnp.where(lane >= base + R, upper, inverse)
        ah, am, al = split3(upper)
        bh, bm, bl = split3(right)
        a = jnp.concatenate([ah, ah, am, am, ah, al], axis=0).astype(jnp.bfloat16)
        b = jnp.concatenate([bh, bm, bh, bm, bl, bh], axis=0).astype(jnp.bfloat16)
        keep = (block_row >= base + R) & (block_lane >= base) & (block_lane < base + R)
        d_ref[...] = jnp.where(keep, 0.0, d_ref[...]) - dot(a, b, TN, None)
        return carry

    lax.fori_loop(0, B // R, panel, 0)


def factor_kernel(n, gram_ref, inv_ref, d_ref, w_ref, m_ref):
    for i in range(n):
        at = B * (i * (i + 1) // 2)
        m_ref[pl.ds(i * B, B), pl.ds(0, (i + 1) * B)] = gram_ref[:, pl.ds(at, (i + 1) * B)]
    for k in range(n):
        rows = pl.ds(k * B, B)
        d_ref[...] = m_ref[rows, rows]
        invert_factor(d_ref, w_ref)
        w = w_ref[...]
        if k:
            inv_ref[rows, pl.ds(0, k * B)] = dot(w, m_ref[rows, pl.ds(0, k * B)], NN)
        inv_ref[rows, rows] = w
        if k + 1 < n:
            rest = (n - 1 - k) * B
            inv_ref[rows, pl.ds((k + 1) * B, rest)] = jnp.zeros((B, rest), jnp.float32)
            below = pl.ds((k + 1) * B, rest)
            panel = dot(m_ref[below, rows], w, NT)
            m_ref[below, rows] = -dot(panel, w, NN)
            if k:
                m_ref[below, pl.ds(0, k * B)] -= dot(panel, inv_ref[rows, pl.ds(0, k * B)], NN)
            for i in range(k + 1, n):
                a = panel[(i - k - 1) * B : (i - k) * B]
                m_ref[pl.ds(i * B, B), pl.ds((k + 1) * B, (i - k) * B)] -= dot(a, panel[: (i - k) * B], NT)


def inverse_factor(packed, width):
    n = width // B
    return pl.pallas_call(
        functools.partial(factor_kernel, n),
        out_shape=jax.ShapeDtypeStruct((width, width), jnp.float32),
        in_specs=[pl.BlockSpec(memory_space=pltpu.VMEM)],
        out_specs=pl.BlockSpec(memory_space=pltpu.VMEM),
        scratch_shapes=[
            pltpu.VMEM((B, B), jnp.float32),
            pltpu.VMEM((B, B), jnp.float32),
            pltpu.VMEM((width, width), jnp.float32),
        ],
        compiler_params=pltpu.CompilerParams(vmem_limit_bytes=32 * 1024 * 1024),
    )(packed)


def reduce_kernel(n, chunks, x_ref, stats_ref, out_ref, all_ref, half_in, half, quarter_in, quarter,
                  far_in, send_sem, recv_sem, stat_send, stat_recv):
    me = lax.axis_index("tm")
    levels = n.bit_length() - 1
    rows = x_ref.shape[0] // chunks
    h, q = rows // 2, rows // 4
    bit0, bit1 = lax.rem(me, 2), lax.rem(me // 2, 2)

    def across(level):
        size = 2**level
        return me + size * (1 - 2 * lax.rem(me // size, 2))

    barrier = pltpu.get_barrier_semaphore()
    for d in range(1, n):
        pl.semaphore_signal(
            barrier, inc=1, device_id={"tm": lax.rem(me + d, n)}, device_id_type=pl.DeviceIdType.MESH
        )
    pl.semaphore_wait(barrier, n - 1)

    def copy(src, dst, peer, ssem, rsem):
        c = pltpu.make_async_remote_copy(
            src_ref=src,
            dst_ref=dst,
            send_sem=ssem,
            recv_sem=rsem,
            device_id={"tm": peer},
            device_id_type=pl.DeviceIdType.MESH,
        )
        c.start()
        return c

    def part(start, size):
        return pl.ds(pl.multiple_of(start, q), size)

    flight = {}
    stages = levels + 2

    def step(c, stage):
        if stage:
            flight[c].wait()
        s0 = c * rows + bit0 * h
        s1 = s0 + bit1 * q
        mine = part(s1, q)
        if stage == 1:
            half[c] = x_ref[part(s0, h), :] + half_in[c]
        elif stage == 2:
            quarter[0, c] = half[c, part(bit1 * q, q), :] + quarter_in[c]
        elif 2 < stage < levels:
            quarter[stage - 2, c] = quarter[stage - 3, c] + far_in[stage - 3, c]
        elif stage == levels:
            out_ref[mine, :] = quarter[levels - 3, c] + far_in[levels - 3, c]
        if stage == stages:
            return
        if stage == 0:
            src, dst, peer = x_ref.at[part(c * rows + (1 - bit0) * h, h)], half_in.at[c], across(0)
        elif stage == 1:
            src, dst, peer = half.at[c, part((1 - bit1) * q, q)], quarter_in.at[c], across(1)
        elif stage < levels:
            src, dst, peer = quarter.at[stage - 2, c], far_in.at[stage - 2, c], across(stage)
        elif stage == levels:
            src, dst, peer = out_ref.at[mine], out_ref.at[mine], across(1)
        else:
            own = part(s0, h)
            src, dst, peer = out_ref.at[own], out_ref.at[own], across(0)
        flight[c] = copy(src, dst, peer, send_sem.at[stage, c], recv_sem.at[stage, c])

    for c in range(chunks):
        step(c, 0)
    all_ref[me] = stats_ref[...]
    gathers = [
        copy(stats_ref, all_ref.at[me], lax.rem(me + d, n), stat_send.at[d], stat_recv.at[d])
        for d in range(1, n)
    ]
    for t in range(1, chunks + stages):
        for c in range(chunks):
            if 1 <= t - c <= stages:
                step(c, t - c)
    for g in gathers:
        g.wait()


def reduce_and_gather(packed, stats, n):
    assert n >= 8 and n & (n - 1) == 0
    chunks = 4
    levels = n.bit_length() - 1
    height, width = packed.shape
    h, q = height // chunks // 2, height // chunks // 4
    f32 = jnp.float32
    vmem = pl.BlockSpec(memory_space=pltpu.VMEM)
    return pl.pallas_call(
        functools.partial(reduce_kernel, n, chunks),
        out_shape=(
            jax.ShapeDtypeStruct((height, width), f32),
            jax.ShapeDtypeStruct((n,) + stats.shape, f32),
        ),
        in_specs=[vmem] * 2,
        out_specs=(vmem, vmem),
        scratch_shapes=[
            pltpu.VMEM((chunks, h, width), f32),
            pltpu.VMEM((chunks, h, width), f32),
            pltpu.VMEM((chunks, q, width), f32),
            pltpu.VMEM((levels - 2, chunks, q, width), f32),
            pltpu.VMEM((levels - 2, chunks, q, width), f32),
            pltpu.SemaphoreType.DMA((levels + 2, chunks)),
            pltpu.SemaphoreType.DMA((levels + 2, chunks)),
            pltpu.SemaphoreType.DMA((n,)),
            pltpu.SemaphoreType.DMA((n,)),
        ],
        compiler_params=pltpu.CompilerParams(
            collective_id=0, has_side_effects=True, vmem_limit_bytes=32 * 1024 * 1024
        ),
    )(packed, stats)


def padded(shard, axis, width):
    count, length = (lax.axis_size(axis), shard.shape[0])
    up = [(i, (i + 1) % count) for i in range(count - 1)]
    down = [(j, i) for i, j in up]
    before = lax.ppermute(shard[length - width :], axis, up)
    after = lax.ppermute(shard[:width], axis, down)
    return jnp.concatenate([before, shard, after], axis=0)


def lower_blocks(rows_of, n):
    return jnp.concatenate([rows_of(i) for i in range(n)], axis=1)


def per_device(frames, conv_weight, conv_bias, proj_weight, frames_before, frames_after):
    local_frames = frames[0]
    frame_rows = local_frames.shape[0]
    width = proj_weight.shape[1]
    n = width // B
    live = (frames_before >= 0).astype(jnp.float32)
    padded_input = padded(local_frames, "tm", DILATION_STEP)
    total = jnp.zeros((frame_rows, local_frames.shape[1]), jnp.float32)
    for frame_index in range(3):
        shift_amount = (frame_index - 1) * DILATION_STEP
        valid = ((frames_before >= -shift_amount) & (frames_after >= shift_amount)).astype(
            jnp.float32
        )
        shifted_input = padded_input[
            DILATION_STEP + shift_amount : DILATION_STEP + shift_amount + frame_rows
        ]
        term = jnp.dot(shifted_input, conv_weight[frame_index], preferred_element_type=jnp.float32)
        total = total + valid[:, None] * term
    hidden = (live[:, None] * jax.nn.gelu(total + conv_bias[None, :], approximate=True)).astype(
        jnp.bfloat16
    )
    embed = jnp.dot(hidden, proj_weight, preferred_element_type=jnp.float32)

    local_count = jnp.sum(live)
    local_mean = jnp.sum(embed, axis=0) / jnp.maximum(local_count, 1.0)
    stats = jnp.concatenate([local_mean, jnp.broadcast_to(local_count, (B,))])[None]
    about = live[:, None] * (embed - local_mean[None, :])
    pair = 2 * B
    bands = [
        dot(about[:, i * pair : (i + 1) * pair], about[:, : (i + 1) * pair], TN) for i in range(n // 2)
    ]
    gram = lower_blocks(
        lambda i: bands[i // 2][(i % 2) * B : (i % 2 + 1) * B, : (i + 1) * B], n
    )
    gram, stats = reduce_and_gather(gram, stats, lax.axis_size("tm"))
    stats = stats[:, 0]
    counts = stats[:, width]
    means = stats[:, :width]
    count = jnp.sum(counts)
    mean = jnp.sum(counts[:, None] * means, axis=0) / count
    offset = jnp.sqrt(counts)[:, None] * (means - mean[None, :])
    between = lower_blocks(
        lambda i: dot(offset[:, i * B : (i + 1) * B], offset[:, : (i + 1) * B], TN), n
    )
    ridge = lower_blocks(lambda i: eps_shrink * jnp.eye(B, (i + 1) * B, i * B, dtype=jnp.float32), n)
    inverse = inverse_factor((gram + between) / count + ridge, width)

    def whiten(start, size):
        rows = lax.dynamic_slice_in_dim(embed, start, size)
        here = lax.dynamic_slice_in_dim(live, start, size)
        return dot(here[:, None] * (rows - mean[None, :]), inverse, NT)

    half = frame_rows // 2
    bit = lax.axis_index("view") % 2
    pairs = [(i, i ^ 1) for i in range(lax.axis_size("view"))]
    first = whiten((1 - bit) * half, half)
    arrived = lax.ppermute(first.astype(jnp.bfloat16), "view", pairs)
    own = whiten(bit * half, half)
    whitened = jnp.where(bit == 0, jnp.concatenate([own, first]), jnp.concatenate([first, own]))
    diff = own - arrived.astype(jnp.float32)
    mine = jnp.sum(diff * diff, axis=1) / width
    theirs = lax.ppermute(mine, "view", pairs)
    pair_loss = jnp.where(bit == 0, jnp.concatenate([mine, theirs]), jnp.concatenate([theirs, mine]))
    return (whitened[None], pair_loss[None])


def solution(mesh):
    return jax.shard_map(
        per_device,
        mesh=mesh,
        in_specs=(P("view", "tm", None), P(), P(), P(), P("tm"), P("tm")),
        out_specs=(P("view", "tm", None), P("view", "tm")),
        check_vma=False,
    )
```
